512 devices in a mesh: dp: 16 (over z), expert: 32 (over x, y, core).
Axes of the slice: x: 4, y: 4, z: 16, core: 2. Of those that a mesh axis runs over, the one named last changes fastest.
Arguments:
- learn_hidden: bfloat16 [16, 128, 32, 1024], P('dp', 'expert'), may hold values from -6 to 6
- learn_cotangent: bfloat16 [16, 128, 32, 4096], P('dp', 'expert'), may hold values from -6 to 6
- master_blocks: float32 [32, 16, 2, 128, 128], P('expert', 'dp'), may hold values from -0.1875 to 0.1875
- changed: int32 [32, 16, 2], replicated, may hold values from 0 to 63, as said below
- rollout_slot: int32 [128], replicated, may hold values from 0 to 127, as said below
- rollout_weight: bfloat16 [128, 1024, 4096], P('expert', None, 'dp'), may hold values from -448 to 448
- rollout_scale: bfloat16 [128, 8, 32], P('expert', None, 'dp'), may hold values from 0.00014972687 to 0.00059890747
- decode_hidden: bfloat16 [2, 2048, 1024], P(None, 'expert'), may hold values from -6 to 6
- decode_routes: int32 [2, 2048, 8], P(None, 'expert'), may hold values from 0 to 127, all different within a row; in each aligned block of 64 rows (0 to 63, 64 to 127, ..., all dimensions but the last counted through in order) at most 8 rows name the same one
- decode_gates: float32 [2, 2048, 8], P(None, 'expert'), may hold values from 0.05 to 0.5
Outputs:
- decode_out: bfloat16 [2, 2048, 4096], P(None, 'expert', 'dp')
The draws below stay inside these ranges and needn't reach their ends.
Inputs may be any that keep to these rules, and one draw needn't show every extreme that they name: `changed`: for each learner index j and group g the 2 codes differ; code k names expert j * 4 + k // 16, block row (k // 2) % 8 and block column g * 2 + k % 2. `rollout_slot`: each expert has its own row. `decode_routes`: each token names 8 different experts. Among the 64 tokens of one index of expert in one step no expert is named by more than 8 tokens, a bound that some block reaches.
All inputs are finite; a program needn't handle non-finite values.
Results may differ from the reference program's by a relative error of at most 0.006.
Values may be sent and summed in bfloat16 or wider, within the bound.
No kernel may reach another device: no remote copies, remote signals or barrier semaphores. Data moves between devices by JAX's collectives and lax.ppermute only.
A program may use at most 64 MiB of HBM per device.

```python
import math
import jax
import jax.numpy as jnp
import numpy as np
from jax import lax

D = 4096
FF = 1024
BLK = 128
TOP = 8
EXP_DEV = 4
LROWS = 32
CBD = 2
TOK_DEV = 64
EXPERTS = 128
TOKENS = 2048
FBR = 8
CAP = 8
N_DP = 16
N_EXPERT = 32


def draw_changed(key, part):
    key = jax.random.fold_in(key, 11)
    block_total = EXP_DEV * (FF // BLK) * (D // BLK // N_DP)
    random_scores = jax.random.randint(key, (N_EXPERT, N_DP, block_total), 0, 1 << 20) * block_total + jnp.arange(block_total, dtype=jnp.int32)
    ranking = jnp.argsort(random_scores, axis=-1)
    return ranking[:, :, :CBD].astype(jnp.int32)


def draw_rollout_slot(key, part):
    key = jax.random.fold_in(key, 23)
    order_key, pick_key = jax.random.split(key)
    ordering = jax.random.permutation(order_key, jnp.arange(EXPERTS, dtype=jnp.int32)).astype(jnp.int32)
    target = (N_EXPERT // 2 * EXP_DEV + jax.random.randint(pick_key, (), 0, EXP_DEV)).astype(jnp.int32)
    located = jnp.argmax((ordering == target).astype(jnp.int32)).astype(jnp.int32)
    first_value = ordering[0]
    ordering = ordering.at[located].set(first_value)
    ordering = ordering.at[0].set(target)
    return ordering.astype(jnp.int32)


def levels(own_key, dims, cuts, least, largest):
    factor_of = 1.0
    for dim, shards_of in cuts:
        draws = jax.random.uniform(jax.random.fold_in(jax.random.fold_in(own_key, 6), dim), (shards_of,), jnp.float32, least / len(cuts), largest / len(cuts))
        factor_of = factor_of * jnp.repeat(jnp.exp(draws), dims[dim] // shards_of).reshape((-1,) + (1,) * (len(dims) - 1 - dim))
    return factor_of


def routed_block(stream_key, own, number, rows, number_of, top, reach, slope):
    sequence = jax.random.permutation(stream_key, number_of)
    heavy_load, usual = portions_of(number_of, rows * top, reach, slope, True), portions_of(number_of, rows * top, reach, slope, False)
    places = jnp.arange(number_of)

    def named(lengths, turn):
        used = int((lengths > 0).sum())
        fixed = max(1, used // 4)
        passed = fixed + (places - fixed + turn * (used - fixed)) % max(1, number_of - fixed)
        return jnp.zeros((number_of,), jnp.int32).at[sequence[jnp.where(places < fixed, places, passed)]].set(jnp.asarray(lengths, jnp.int32))

    lengths = jnp.where(number % 4 == 0, named(heavy_load, number // 4), named(usual, number - number // 4 - 1))
    mixed = jax.random.permutation(jax.random.fold_in(own, 3), number_of)
    donor, sink = mixed[0:number_of // 2 * 2:2], mixed[1:number_of // 2 * 2:2]
    margin = jnp.minimum(lengths[donor] - 1, reach - lengths[sink]) // 2
    margin = jnp.where((donor == sequence[0]) | (sink == sequence[0]) | (lengths[sink] == 0), 0, jnp.maximum(margin, 0))
    passed = jax.random.randint(jax.random.fold_in(own, 4), (number_of // 2,), 0, 1 << 20) % (margin + 1)
    lengths = lengths.at[donor].add(-passed).at[sink].add(passed)
    labels = jnp.searchsorted(jnp.cumsum(lengths), jnp.arange(rows * top), side="right").astype(jnp.int32)
    table = labels.reshape(top, rows).T
    table = table[jax.random.permutation(jax.random.fold_in(own, 1), rows)]
    turn = jax.random.randint(jax.random.fold_in(own, 2), (rows, 1), 0, top)
    return jnp.take_along_axis(table, (jnp.arange(top)[None, :] + turn) % top, axis=1)


def portions_of(number_of, total, most, slope, full):
    loads = [(1 << 20) // math.isqrt(rank ** slope) + 1 for rank in range(1, number_of + 1)]
    largest = most if full else min(most, max(-(-total // number_of), total * loads[0] // sum(loads)))
    least = 1 if total - largest >= number_of - 1 else 0
    holding, rest = [largest] + [least] * (number_of - 1), total - largest - least * (number_of - 1)
    while rest > 0:
        free = [i for i in range(1, number_of) if holding[i] < largest] or [i for i in range(1, number_of) if holding[i] < most]
        pool, remaining = sum([loads[i] for i in free]), rest
        for i in free:
            extra = min(most - holding[i], max(1, remaining * loads[i] // pool), rest)
            holding[i] = holding[i] + extra
            rest = rest - extra
    return np.array(holding)


def gaussian(key, dims, width, reach, cuts=(), kind=jnp.bfloat16):
    array = width * jax.random.normal(key, dims, jnp.float32)
    if cuts:
        array = array * levels(key, dims, cuts, -0.22, 0.18)
    return jnp.clip(array, -reach, reach).astype(kind)


def setup_inputs(seed: int = 0) -> dict:
    seeds = jax.random.split(jax.random.key(seed), 11)
    learn_hidden = gaussian(seeds[0], (N_DP, EXPERTS, LROWS, FF), 1.0, 6.0, ((0, 16), (1, 32)))
    learn_cotangent = gaussian(seeds[1], (N_DP, EXPERTS, LROWS, D), 1.0, 6.0, ((0, 16), (1, 32)))
    master_blocks = gaussian(seeds[2], (N_EXPERT, N_DP, CBD, BLK, BLK), FF ** -0.5, 0.1875, ((0, 32), (1, 16)), jnp.float32)
    changed = draw_changed(jax.random.fold_in(seeds[10], 71), 0)
    rollout_slot = draw_rollout_slot(jax.random.fold_in(seeds[10], 71), 0)
    rollout_weight = gaussian(seeds[5], (EXPERTS, FF, D), 100.0, 448.0, ((0, 32), (2, 16)))
    rollout_scale = jnp.clip(jnp.exp(math.log(0.00059890747) - 1.3862944 * jax.random.uniform(seeds[6], (EXPERTS, FBR, D // BLK), jnp.float32) ** levels(seeds[6], (EXPERTS, FBR, D // BLK), ((0, 32), (2, 16)), -0.2, 0.2)), 0.00014972687, 0.00059890747).astype(jnp.bfloat16)
    decode_hidden = gaussian(seeds[7], (2, TOKENS, FF), 1.0, 6.0, ((1, 32),))
    decode_routes_keys = jax.random.split(jax.random.fold_in(seeds[8], 1), 2 * TOKENS // TOK_DEV)
    decode_routes_turns = jax.random.permutation(jax.random.fold_in(seeds[8], 3), 2 * TOKENS // TOK_DEV)
    decode_routes = jax.vmap(lambda own, number: routed_block(jax.random.fold_in(seeds[8], 2), own, number, TOK_DEV, EXPERTS, TOP, CAP, 2))(decode_routes_keys, decode_routes_turns).reshape((2, TOKENS, TOP))
    decode_gates = jnp.clip(jnp.exp(math.log(0.5) - 2.3025851 * jax.random.uniform(seeds[9], (2, TOKENS, TOP), jnp.float32) ** levels(seeds[9], (2, TOKENS, TOP), ((1, 32),), -0.2, 0.2)), 0.05, 0.5)
    return dict(learn_hidden=learn_hidden, learn_cotangent=learn_cotangent, master_blocks=master_blocks, changed=changed, rollout_slot=rollout_slot, rollout_weight=rollout_weight, rollout_scale=rollout_scale, decode_hidden=decode_hidden, decode_routes=decode_routes, decode_gates=decode_gates)


learning_rate = 0.03
quant_limit = 448.0
epsilon_value = 1e-06

def quantize(updated):
    peak = lax.optimization_barrier(jnp.max(jnp.abs(updated), axis=(-2, -1)))
    block_scale = ((peak + epsilon_value) / quant_limit).astype(jnp.bfloat16)
    packed = (updated / block_scale.astype(jnp.float32)[..., None, None]).astype(jnp.bfloat16)
    return (packed, block_scale)

def reference(learn_hidden, learn_cotangent, master_blocks, changed, rollout_slot, rollout_weight, rollout_scale, decode_hidden, decode_routes, decode_gates):
    row_blocks = FF // BLK
    col_blocks = D // BLK
    col_local = col_blocks // N_DP
    step_size = learning_rate / math.sqrt(N_DP * LROWS)
    column_group = jnp.arange(N_DP, dtype=jnp.int32)[:, None]

    def per_learner(learner):
        hidden_part = lax.dynamic_slice_in_dim(learn_hidden, learner * EXP_DEV, EXP_DEV, 1)
        cotangent_part = lax.dynamic_slice_in_dim(learn_cotangent, learner * EXP_DEV, EXP_DEV, 1)
        hidden_tiles = hidden_part.reshape(N_DP, EXP_DEV, LROWS, row_blocks, BLK).transpose(1, 3, 0, 2, 4).reshape(EXP_DEV * row_blocks, N_DP * LROWS, BLK)
        cotangent_tiles = cotangent_part.reshape(N_DP, EXP_DEV, LROWS, col_blocks, BLK).transpose(1, 3, 0, 2, 4).reshape(EXP_DEV * col_blocks, N_DP * LROWS, BLK)
        block_code = changed[learner]
        local_expert = block_code // (row_blocks * col_local)
        block_row = block_code // col_local % row_blocks
        block_col = column_group * col_local + block_code % col_local
        left = hidden_tiles[local_expert * row_blocks + block_row].astype(jnp.float32)
        right = cotangent_tiles[local_expert * col_blocks + block_col].astype(jnp.float32)
        gradient = jnp.einsum('gcrp,gcrq->gcpq', left, right)
        updated = master_blocks[learner] - step_size * gradient
        return quantize(updated)
    packed, block_scale = lax.map(per_learner, jnp.arange(N_EXPERT, dtype=jnp.int32))
    learner_ids = jnp.arange(N_EXPERT, dtype=jnp.int32)[:, None, None]
    local_expert = changed // (row_blocks * col_local)
    block_row = changed // col_local % row_blocks
    block_col = jnp.arange(N_DP, dtype=jnp.int32)[None, :, None] * col_local + changed % col_local
    position = rollout_slot[learner_ids * EXP_DEV + local_expert]
    weights = rollout_weight.reshape(EXPERTS, row_blocks, BLK, col_blocks, BLK)
    weights = weights.at[position, block_row, :, block_col, :].set(packed)
    weights = weights.reshape(EXPERTS, row_blocks, BLK, D)
    scales = rollout_scale.at[position, block_row, block_col].set(block_scale)
    scale_cols = jnp.repeat(scales.astype(jnp.float32), BLK, axis=2)
    most = CAP * N_EXPERT

    def decode_once(hidden, routes, gates):
        flattened = routes.reshape(-1)
        flat_gates = gates.reshape(-1)

        def per_expert(total, expert):
            found = jnp.nonzero(flattened == expert, size=most, fill_value=-1)[0].astype(jnp.int32)
            is_valid = found >= 0
            which_pair = jnp.where(is_valid, found, 0).astype(jnp.int32)
            token_row = which_pair // TOP
            row_data = hidden[token_row].astype(jnp.float32).reshape(most, row_blocks, BLK)
            position_now = rollout_slot[expert]
            matrix = weights[position_now].astype(jnp.float32)
            partial_value = jnp.einsum('rbf,bfc->rbc', row_data, matrix)
            expert_rows = lax.optimization_barrier(jnp.sum(partial_value * scale_cols[position_now][None], axis=1)).astype(jnp.bfloat16)
            added = jnp.where(is_valid[:, None], flat_gates[which_pair][:, None] * expert_rows.astype(jnp.float32), jnp.float32(0.0))
            return (total.at[token_row].add(added), None)
        total, _ = lax.scan(per_expert, jnp.zeros((TOKENS, D), jnp.float32), jnp.arange(EXPERTS, dtype=jnp.int32))
        return total.astype(jnp.bfloat16)
    return jnp.stack([decode_once(decode_hidden[section_index], decode_routes[section_index], decode_gates[section_index]) for section_index in range(2)])
```

```python
import functools
import math

import jax
import jax.numpy as jnp
from jax import lax
from jax.experimental import pallas as pl
from jax.experimental.pallas import tpu as pltpu
from jax.sharding import PartitionSpec as P

learning_rate = 0.03
quant_limit = 448.0
epsilon_value = 1e-06

SIDE = 4
CORES = 2
BLK = 128
SHIFTS = (1, 3, 2)
VMEM = pltpu.VMEM
SMEM = pltpu.SMEM


def vmem():
    return pl.BlockSpec(memory_space=VMEM)


def smem():
    return pl.BlockSpec(memory_space=SMEM)


def line_shift(stage, shift):
    pairs = []
    for x in range(SIDE):
        for y in range(SIDE):
            for core in range(CORES):
                if (core == 0) == (stage == 0):
                    to = (x, (y + shift) % SIDE)
                else:
                    to = ((x + shift) % SIDE, y)
                pairs.append(((x * SIDE + y) * CORES + core, (to[0] * SIDE + to[1]) * CORES + core))
    return pairs


def core_swap():
    return [(i, i ^ 1) for i in range(SIDE * SIDE * CORES)]


def same_core():
    return [[2 * i + core for i in range(SIDE * SIDE)] for core in range(CORES)]


def select_kernel(code_ref, hidden_ref, cotangent_ref, out_ref):
    groups, per_group = out_ref.shape[0], out_ref.shape[1]
    for g in range(groups):
        for c in range(per_group):
            k = code_ref[g * per_group + c]
            e = k >> 4
            r = (k >> 1) & 7
            b = (k & 1) + 2 * g
            out_ref[g, c, 0] = hidden_ref[e, :, pl.ds(pl.multiple_of(r * BLK, BLK), BLK)]
            out_ref[g, c, 1] = cotangent_ref[e, :, pl.ds(pl.multiple_of(b * BLK, BLK), BLK)]


def chunk_kernel(token_ref, route_ref, gate_ref, out_ref):
    tokens = token_ref.shape[0] * token_ref.shape[1]
    top = route_ref.shape[2]
    out_ref[0:tokens, :] = token_ref[...].reshape(tokens, token_ref.shape[2])
    route = route_ref[...].reshape(tokens, top).astype(jnp.float32)
    gate = gate_ref[...].reshape(tokens, top)
    high = gate.astype(jnp.bfloat16)
    low = (gate - high.astype(jnp.float32)).astype(jnp.bfloat16)
    same = lax.broadcasted_iota(jnp.int32, (tokens, tokens), 0) == lax.broadcasted_iota(
        jnp.int32, (tokens, tokens), 1
    )
    eye = same.astype(jnp.float32).astype(jnp.bfloat16)

    def turned(v):
        return lax.dot_general(
            v, eye, (((0,), (0,)), ((), ())), preferred_element_type=jnp.float32
        )

    out_ref[tokens : tokens + 16, 0:BLK] = jnp.concatenate(
        [turned(route.astype(jnp.bfloat16)), turned(high)], axis=0
    ).astype(jnp.bfloat16)
    out_ref[tokens : tokens + 16, BLK : 2 * BLK] = jnp.concatenate(
        [turned(low), jnp.zeros((8, BLK), jnp.float32)], axis=0
    ).astype(jnp.bfloat16)
    out_ref[tokens : tokens + 16, 2 * BLK :] = jnp.zeros(
        (16, out_ref.shape[1] - 2 * BLK), jnp.bfloat16
    )


def gate_columns(x_ref, q, ids):
    extra = x_ref[q, 128:144, 0 : 2 * BLK].astype(jnp.float32)
    route = extra[0:8, 0:BLK]
    gate = extra[8:16, 0:BLK] + extra[0:8, BLK : 2 * BLK]
    rows = [
        jnp.sum(jnp.where(route == e.astype(jnp.float32), gate, 0.0), axis=0, keepdims=True)
        for e in ids
    ]
    rows.append(jnp.zeros((16 - len(ids), BLK), jnp.float32))
    return jnp.transpose(jnp.concatenate(rows, axis=0))


def main_kernel(id_ref, x_ref, own_ref, other_ref, out_ref, picked_ref):
    chunks = x_ref.shape[0]
    rows = chunks * BLK
    ids = [id_ref[i] for i in range(12)]
    columns = jnp.concatenate([gate_columns(x_ref, q, ids) for q in range(chunks)], axis=0)
    x = x_ref[:, 0:BLK, :].reshape(rows, x_ref.shape[2])
    total = None
    for e in range(8):
        weight = own_ref[e] if e < 4 else other_ref[e - 4]
        part = jnp.dot(x, weight, preferred_element_type=jnp.float32) * columns[:, e : e + 1]
        total = part if total is None else total + part
    out_ref[...] = total
    for c in range(4):
        r = id_ref[12 + c]
        tile = x_ref[:, 0:BLK, pl.ds(pl.multiple_of(r * BLK, BLK), BLK)].reshape(rows, BLK)
        gated = tile.astype(jnp.float32) * columns[:, 8 + c : 9 + c]
        picked_ref[c] = gated.astype(jnp.bfloat16)


def refresh_kernel(recv_ref, master_ref, out_ref, *, step_size):
    groups, per_group = recv_ref.shape[0], recv_ref.shape[1]
    rows = groups * recv_ref.shape[3]
    for c in range(per_group):
        left = recv_ref[:, c, 0].reshape(rows, BLK)
        right = recv_ref[:, c, 1].reshape(rows, BLK)
        gradient = lax.dot_general(
            left, right, (((0,), (0,)), ((), ())), preferred_element_type=jnp.float32
        )
        updated = master_ref[c] - step_size * gradient
        peak = jnp.max(jnp.max(jnp.abs(updated), axis=0, keepdims=True), axis=1, keepdims=True)
        scale = ((peak + epsilon_value) / quant_limit).astype(jnp.bfloat16)
        scale = jnp.broadcast_to(scale.astype(jnp.float32), (16, BLK))
        out_ref[c, 0:BLK, :] = (updated / scale[0:1, :]).astype(jnp.bfloat16)
        out_ref[c, BLK : BLK + 16, :] = scale.astype(jnp.bfloat16)


def combine_kernel(
    place_ref, own_ref, other_ref, m0, m1, m2, m3, p0, p1, p2, p3, out_ref, total
):
    for i, (m_ref, p_ref) in enumerate(((m0, p0), (m1, p1), (m2, p2), (m3, p3))):
        total[...] = m_ref[...]
        for c in range(4):
            block = own_ref[c] if c < 2 else other_ref[c - 2]
            scale = block[BLK : BLK + 16].astype(jnp.float32)[0:1]
            delta = (
                jnp.dot(p_ref[c], block[0:BLK], preferred_element_type=jnp.float32) * scale
            )
            at = pl.ds(pl.multiple_of(place_ref[16 + c] * BLK, BLK), BLK)
            total[:, at] += delta
        for q in range(4):
            out_ref[place_ref[4 * i + q]] = total[q * BLK : (q + 1) * BLK, :].astype(jnp.bfloat16)


def shards(
    learn_hidden,
    learn_cotangent,
    master_blocks,
    changed,
    rollout_slot,
    rollout_weight,
    rollout_scale,
    decode_hidden,
    decode_routes,
    decode_gates,
):
    dp_count = lax.axis_size("dp")
    dp_index = lax.axis_index("dp")
    me = lax.axis_index("expert")
    exp_dev, learn_rows, width_ff = learn_hidden.shape[1:]
    width_local = rollout_weight.shape[2]
    per_group = master_blocks.shape[2]
    row_blocks = width_ff // BLK
    tokens = decode_hidden.shape[0] * decode_hidden.shape[1]
    big = pltpu.CompilerParams(vmem_limit_bytes=40 * 1024 * 1024)

    codes = lax.dynamic_index_in_dim(changed, me, 0, keepdims=False).reshape(-1)
    tiles = pl.pallas_call(
        select_kernel,
        out_shape=jax.ShapeDtypeStruct((dp_count, per_group, 2, learn_rows, BLK), jnp.bfloat16),
        in_specs=[smem(), vmem(), vmem()],
        out_specs=vmem(),
        compiler_params=big,
    )(codes, learn_hidden[0], learn_cotangent[0])
    received = lax.all_to_all(tiles, "dp", 0, 0, tiled=True)

    chunk = pl.pallas_call(
        chunk_kernel,
        out_shape=jax.ShapeDtypeStruct((tokens + 16, width_ff), jnp.bfloat16),
        in_specs=[vmem()] * 3,
        out_specs=vmem(),
    )(decode_hidden, decode_routes, decode_gates)
    line = [chunk] + [lax.ppermute(chunk, "expert", line_shift(0, s)) for s in SHIFTS]
    line = jnp.stack(line)
    pieces = [line] + [lax.ppermute(line, "expert", line_shift(1, s)) for s in SHIFTS]

    experts_all = rollout_slot.shape[0]
    chip = me // CORES
    own_first = jnp.arange(CORES * exp_dev, dtype=jnp.int32)
    position = (me ^ (own_first // exp_dev)) * exp_dev + own_first % exp_dev
    expert_of = jnp.sum(
        jnp.where(
            rollout_slot[None, :] == position[:, None],
            jnp.arange(experts_all, dtype=jnp.int32)[None, :],
            0,
        ),
        axis=1,
    )
    here = lax.dynamic_index_in_dim(changed, dp_index, 1, keepdims=False)
    here_expert = jnp.arange(here.shape[0], dtype=jnp.int32)[:, None] * exp_dev + (here >> 4)
    where_hit = (
        (here_expert.reshape(-1) == expert_of[:exp_dev, None, None, None])
        & ((here.reshape(-1) & 15) == (jnp.arange(row_blocks, dtype=jnp.int32)[:, None, None] * 2
                                       + jnp.arange(2, dtype=jnp.int32)[:, None]))
    )
    replaced = jnp.any(where_hit, axis=-1)
    kept = jnp.where(replaced, 0.0, rollout_scale.astype(jnp.float32))
    scale_cols = jnp.repeat(kept, BLK, axis=2)
    own_weight = (
        rollout_weight.reshape(exp_dev, row_blocks, BLK, width_local).astype(jnp.float32)
        * scale_cols[:, :, None, :]
    ).astype(jnp.bfloat16).reshape(exp_dev, width_ff, width_local)
    other_weight = lax.ppermute(own_weight, "expert", core_swap())

    pair = jnp.stack([me, me ^ 1])
    pair_codes = jnp.take(here, pair, axis=0)
    pair_expert = (pair[:, None] * exp_dev + (pair_codes >> 4)).reshape(-1)
    ids = jnp.concatenate([expert_of, pair_expert, ((pair_codes >> 1) & 7).reshape(-1)])

    rows = SIDE * tokens
    parts = [
        pl.pallas_call(
            main_kernel,
            out_shape=(
                jax.ShapeDtypeStruct((rows, width_local), jnp.float32),
                jax.ShapeDtypeStruct((4, rows, BLK), jnp.bfloat16),
            ),
            in_specs=[smem(), vmem(), vmem(), vmem()],
            out_specs=(vmem(), vmem()),
            compiler_params=big,
            cost_estimate=pl.CostEstimate(
                flops=2 * rows * width_ff * width_local * 8,
                bytes_accessed=8 * 1024 * 1024,
                transcendentals=0,
            ),
        )(ids, piece, own_weight, other_weight)
        for piece in pieces
    ]

    step_size = learning_rate / math.sqrt(dp_count * learn_rows)
    own_block = pl.pallas_call(
        functools.partial(refresh_kernel, step_size=step_size),
        out_shape=jax.ShapeDtypeStruct((per_group, BLK + 16, BLK), jnp.bfloat16),
        in_specs=[vmem(), vmem()],
        out_specs=vmem(),
    )(received, master_blocks[0, 0])
    other_block = lax.ppermute(own_block, "expert", core_swap())

    x, y, core = chip // SIDE, chip % SIDE, me % CORES
    shifts = jnp.array((0,) + SHIFTS, jnp.int32)
    second, first = shifts[:, None], shifts[None, :]
    from_x = (x + SIDE - jnp.where(core == 0, second, first)) % SIDE
    from_y = (y + SIDE - jnp.where(core == 0, first, second)) % SIDE
    place = jnp.concatenate([(from_x * SIDE + from_y).reshape(-1), (pair_codes & 1).reshape(-1)])
    outgoing = pl.pallas_call(
        combine_kernel,
        out_shape=jax.ShapeDtypeStruct((SIDE * SIDE, tokens, width_local), jnp.bfloat16),
        in_specs=[smem()] + [vmem()] * 10,
        out_specs=vmem(),
        scratch_shapes=[pltpu.VMEM((rows, width_local), jnp.float32)],
        compiler_params=big,
    )(place, own_block, other_block, *[p[0] for p in parts], *[p[1] for p in parts])

    returned = lax.all_to_all(
        outgoing, "expert", 0, 0, axis_index_groups=same_core(), tiled=True
    )
    result = jnp.sum(returned.astype(jnp.float32), axis=0).astype(jnp.bfloat16)
    return result.reshape(decode_hidden.shape[0], decode_hidden.shape[1], width_local)


def solution(mesh):
    return jax.shard_map(
        shards,
        mesh=mesh,
        in_specs=(
            P("dp", "expert", None, None),
            P("dp", "expert", None, None),
            P("expert", "dp", None, None, None),
            P(),
            P(),
            P("expert", None, "dp"),
            P("expert", None, "dp"),
            P(None, "expert", None),
            P(None, "expert", None),
            P(None, "expert", None),
        ),
        out_specs=P(None, "expert", "dp"),
        check_vma=False,
    )
```

```python
import functools
import math

import jax
import jax.numpy as jnp
from jax import lax
from jax.experimental import pallas as pl
from jax.experimental.pallas import tpu as pltpu
from jax.sharding import PartitionSpec as P

learning_rate = 0.03
quant_limit = 448.0
epsilon_value = 1e-06

SIDE = 4
CORES = 2
BLK = 128
EXTRA = 32
TURNS = (0, 1, 3, 2)
ANY = pl.ANY
VMEM = pltpu.VMEM
SMEM = pltpu.SMEM


def vmem():
    return pl.BlockSpec(memory_space=VMEM)


def smem():
    return pl.BlockSpec(memory_space=SMEM)


def shifted(stage, shift):
    pairs = []
    for x in range(SIDE):
        for y in range(SIDE):
            here = (x * SIDE + y) * CORES
            along_x = ((x + shift) % SIDE * SIDE + y) * CORES
            along_y = (x * SIDE + (y + shift) % SIDE) * CORES
            first, second = (along_y, along_x) if stage == 0 else (along_x, along_y)
            pairs += [(here, first), (here + 1, second + 1)]
    return pairs


def core_swap():
    return [(i, i ^ 1) for i in range(SIDE * SIDE * CORES)]


def both_cores():
    return [[CORES * i, CORES * i + 1] for i in range(SIDE * SIDE)]


def same_core():
    return [[2 * i + core for i in range(SIDE * SIDE)] for core in range(CORES)]


def select_kernel(changed_ref, hidden_ref, cotangent_ref, out_ref, sems):
    me = lax.axis_index("expert")
    groups, per_group = out_ref.shape[0], out_ref.shape[1]
    copies = []
    for g in range(groups):
        for c in range(per_group):
            k = changed_ref[g, c, me]
            e = k >> 4
            r = (k >> 1) & 7
            b = (k & 1) + 2 * g
            for i, (ref, block) in enumerate(((hidden_ref, r), (cotangent_ref, b))):
                copy = pltpu.make_async_copy(
                    ref.at[e, :, pl.ds(pl.multiple_of(block * BLK, BLK), BLK)],
                    out_ref.at[g, c, i],
                    sems.at[g, c, i],
                )
                copy.start()
                copies.append(copy)
    for copy in copies:
        copy.wait()


def chunk_kernel(slot_ref, token_ref, route_ref, gate_ref, out_ref):
    steps, per_step, width = token_ref.shape
    tokens = steps * per_step
    blocks = width // BLK
    route = jnp.concatenate([route_ref[s] for s in range(steps)], axis=1)
    place = jnp.zeros_like(route)
    for e in range(slot_ref.shape[0]):
        place = jnp.where(route == e, slot_ref[e], place)
    gate = jnp.concatenate([gate_ref[s] for s in range(steps)], axis=1)
    high = gate.astype(jnp.bfloat16).astype(jnp.float32)
    low = (gate - high).astype(jnp.bfloat16).astype(jnp.float32)
    extra = jnp.concatenate([place.astype(jnp.float32), high, low, jnp.zeros_like(low)], axis=0)
    extra = extra.astype(jnp.bfloat16)
    for r in range(blocks):
        tile = token_ref[:, :, r * BLK : (r + 1) * BLK].reshape(tokens, BLK)
        out_ref[r * BLK : (r + 1) * BLK, :] = tile
    out_ref[blocks * BLK :, :] = extra


def weight_kernel(changed_ref, slot_ref, scale_ref, own_ref, other_ref, out_ref, kept):
    me, g = lax.axis_index("expert"), lax.axis_index("dp")
    chip = me // CORES
    exp_dev = own_ref.shape[0]
    held, per_expert = scale_ref.shape
    for s in range(held):
        for n in range(per_expert):
            kept[s, n] = scale_ref[s, n]
    for j in range(changed_ref.shape[2]):
        for c in range(changed_ref.shape[1]):
            k = changed_ref[g, c, j]
            place = slot_ref[j * exp_dev + (k >> 4)]

            @pl.when(place // held == chip)
            def _():
                kept[place % held, k & 15] = 0.0

    for h, ref in enumerate((own_ref, other_ref)):
        first = ((me + h) % CORES) * exp_dev
        for s in range(exp_dev):
            for n in range(per_expert):
                rows, columns = pl.ds(n // 2 * BLK, BLK), pl.ds(n % 2 * BLK, BLK)
                scaled = ref[s, rows, columns].astype(jnp.float32) * kept[first + s, n]
                out_ref[h * exp_dev + s, rows, columns] = scaled.astype(jnp.bfloat16)


def gate_columns(x_ref, places):
    base = x_ref.shape[1] - EXTRA
    columns = []
    for q in range(x_ref.shape[0]):
        extra = x_ref[q, base : base + EXTRA, :].astype(jnp.float32)
        place = extra[0:8]
        gate = extra[8:16] + extra[16:24]
        rows = [
            jnp.sum(jnp.where(place == p.astype(jnp.float32), gate, 0.0), axis=0, keepdims=True)
            for p in places
        ]
        rows.append(jnp.zeros((16 - len(places), BLK), jnp.float32))
        columns.append(jnp.transpose(jnp.concatenate(rows, axis=0)))
    return jnp.concatenate(columns, axis=0)


def line_sum(changed_ref, slot_ref, block_ref, weight_ref, x_ref, total):
    me, g = lax.axis_index("expert"), lax.axis_index("dp")
    chip = me // CORES
    held = weight_ref.shape[0]
    exp_dev = held // CORES
    rows = x_ref.shape[0] * BLK
    codes = [changed_ref[g, c % 2, chip * CORES + c // 2] for c in range(4)]
    places = [me * exp_dev + e for e in range(exp_dev)]
    places += [(me ^ 1) * exp_dev + e for e in range(exp_dev)]
    places += [slot_ref[(chip * CORES + c // 2) * exp_dev + (codes[c] >> 4)] for c in range(4)]
    columns = gate_columns(x_ref, places)
    x = jnp.concatenate(
        [
            x_ref[:, r * BLK : (r + 1) * BLK, :].reshape(rows, BLK)
            for r in range(weight_ref.shape[1] // BLK)
        ],
        axis=1,
    )
    value = None
    for e in range(held):
        part = jnp.dot(x, weight_ref[e], preferred_element_type=jnp.float32)
        part = part * columns[:, e : e + 1]
        value = part if value is None else value + part
    total[...] = value
    for c in range(4):
        r = (codes[c] >> 1) & 7
        tile = x_ref[:, pl.ds(pl.multiple_of(r * BLK, BLK), BLK), :].reshape(rows, BLK)
        scale = block_ref[c, BLK : BLK + 16, :].astype(jnp.float32)[0:1, 0:1]
        delta = jnp.dot(tile, block_ref[c, 0:BLK, :], preferred_element_type=jnp.float32)
        at = pl.ds(pl.multiple_of((codes[c] & 1) * BLK, BLK), BLK)
        total[:, at] += delta * (scale * columns[:, held + c : held + c + 1])


def line_kernel(changed_ref, slot_ref, block_ref, weight_ref, x_ref, out_ref, total):
    line_sum(changed_ref, slot_ref, block_ref, weight_ref, x_ref, total)
    out_ref[...] = total[...].astype(jnp.bfloat16)


def refresh_kernel(recv_ref, master_ref, out_ref, *, step_size):
    groups, per_group = recv_ref.shape[0], recv_ref.shape[1]
    rows = groups * recv_ref.shape[3]
    for c in range(per_group):
        left = recv_ref[:, c, 0].reshape(rows, BLK)
        right = recv_ref[:, c, 1].reshape(rows, BLK)
        gradient = lax.dot_general(
            left, right, (((0,), (0,)), ((), ())), preferred_element_type=jnp.float32
        )
        updated = master_ref[c] - step_size * gradient
        peak = jnp.max(jnp.max(jnp.abs(updated), axis=0, keepdims=True), axis=1, keepdims=True)
        scale = ((peak + epsilon_value) / quant_limit).astype(jnp.bfloat16)
        scale = jnp.broadcast_to(scale.astype(jnp.float32), (16, BLK))
        out_ref[c, 0:BLK, :] = (updated / scale[0:1, :]).astype(jnp.bfloat16)
        out_ref[c, BLK : BLK + 16, :] = scale.astype(jnp.bfloat16)


def last_kernel(
    changed_ref, slot_ref, block_ref, weight_ref, x_ref, d0, d1, d2, out_ref, total
):
    me = lax.axis_index("expert")
    chip, core = me // CORES, me % CORES
    x, y = chip // SIDE, chip % SIDE
    line_sum(changed_ref, slot_ref, block_ref, weight_ref, x_ref, total)
    for ref, second in zip((d0, d1, d2, total), TURNS):
        for q, first in enumerate(TURNS):
            x_back = jnp.where(core == 0, second, first)
            y_back = jnp.where(core == 0, first, second)
            to = (x + SIDE - x_back) % SIDE * SIDE + (y + SIDE - y_back) % SIDE
            out_ref[to] = ref[q * BLK : (q + 1) * BLK, :].astype(jnp.bfloat16)


def shards(
    learn_hidden,
    learn_cotangent,
    master_blocks,
    changed,
    rollout_slot,
    rollout_weight,
    rollout_scale,
    decode_hidden,
    decode_routes,
    decode_gates,
):
    dp_count = lax.axis_size("dp")
    exp_dev, learn_rows, width_ff = learn_hidden.shape[1:]
    width_local = rollout_weight.shape[2]
    per_group = master_blocks.shape[2]
    tokens = decode_hidden.shape[0] * decode_hidden.shape[1]
    rows = SIDE * tokens
    limit = pltpu.CompilerParams(vmem_limit_bytes=24 * 1024 * 1024)
    table = jnp.transpose(changed, (1, 2, 0))

    tiles = pl.pallas_call(
        select_kernel,
        out_shape=jax.ShapeDtypeStruct((dp_count, per_group, 2, learn_rows, BLK), jnp.bfloat16),
        in_specs=[smem()] + [pl.BlockSpec(memory_space=ANY)] * 2,
        out_specs=vmem(),
        scratch_shapes=[pltpu.SemaphoreType.DMA((dp_count, per_group, 2))],
        compiler_params=limit,
    )(table, learn_hidden[0], learn_cotangent[0])
    tiles, decode_hidden = lax.optimization_barrier((tiles, decode_hidden))
    received = lax.all_to_all(tiles, "dp", 0, 0, tiled=True)

    chunk = pl.pallas_call(
        chunk_kernel,
        out_shape=jax.ShapeDtypeStruct((width_ff + EXTRA, BLK), jnp.bfloat16),
        in_specs=[smem()] + [vmem()] * 3,
        out_specs=vmem(),
        compiler_params=limit,
    )(
        rollout_slot,
        decode_hidden,
        jnp.transpose(decode_routes, (0, 2, 1)),
        jnp.transpose(decode_gates, (0, 2, 1)),
    )
    line = jnp.stack(
        [chunk] + [lax.ppermute(chunk, "expert", shifted(0, turn)) for turn in TURNS[1:]]
    )

    right, left, far = [lax.ppermute(line, "expert", shifted(1, turn)) for turn in TURNS[1:]]

    other_weight = lax.ppermute(rollout_weight, "expert", core_swap())
    line, rollout_scale = lax.optimization_barrier((line, rollout_scale))
    scales = lax.all_gather(
        rollout_scale, "expert", axis_index_groups=both_cores(), tiled=True
    )
    weights = pl.pallas_call(
        weight_kernel,
        out_shape=jax.ShapeDtypeStruct((CORES * exp_dev,) + rollout_weight.shape[1:], jnp.bfloat16),
        in_specs=[smem()] * 3 + [vmem()] * 2,
        out_specs=vmem(),
        scratch_shapes=[pltpu.SMEM((CORES * exp_dev, 16), jnp.float32)],
        compiler_params=limit,
    )(
        table,
        rollout_slot,
        scales.astype(jnp.float32).reshape(CORES * exp_dev, -1),
        rollout_weight,
        other_weight,
    )

    step_size = learning_rate / math.sqrt(dp_count * learn_rows)
    own_block = pl.pallas_call(
        functools.partial(refresh_kernel, step_size=step_size),
        out_shape=jax.ShapeDtypeStruct((per_group, BLK + 16, BLK), jnp.bfloat16),
        in_specs=[vmem(), vmem()],
        out_specs=vmem(),
        compiler_params=limit,
    )(received, master_blocks[0, 0])
    blocks = lax.all_gather(own_block, "expert", axis_index_groups=both_cores(), tiled=True)

    def add_up(kernel, out_shape, piece, *done):
        return pl.pallas_call(
            kernel,
            out_shape=jax.ShapeDtypeStruct(out_shape, jnp.bfloat16),
            in_specs=[smem()] * 2 + [vmem()] * (3 + len(done)),
            out_specs=vmem(),
            scratch_shapes=[pltpu.VMEM((rows, width_local), jnp.float32)],
            compiler_params=limit,
            cost_estimate=pl.CostEstimate(
                flops=2 * rows * width_ff * width_local * 8,
                bytes_accessed=6 * 1024 * 1024,
                transcendentals=0,
            ),
        )(table, rollout_slot, blocks, weights, piece, *done)

    done_line = add_up(line_kernel, (rows, width_local), line)
    right, done_line = lax.optimization_barrier((right, done_line))
    done_right = add_up(line_kernel, (rows, width_local), right)
    left, done_right = lax.optimization_barrier((left, done_right))
    done_left = add_up(line_kernel, (rows, width_local), left)
    far, done_left = lax.optimization_barrier((far, done_left))
    outgoing = add_up(
        last_kernel, (SIDE * SIDE, tokens, width_local), far, done_line, done_right, done_left
    )

    returned = lax.all_to_all(
        outgoing, "expert", 0, 0, axis_index_groups=same_core(), tiled=True
    )
    result = jnp.sum(returned.astype(jnp.float32), axis=0).astype(jnp.bfloat16)
    return result.reshape(decode_hidden.shape[0], decode_hidden.shape[1], width_local)


def solution(mesh):
    return jax.shard_map(
        shards,
        mesh=mesh,
        in_specs=(
            P("dp", "expert", None, None),
            P("dp", "expert", None, None),
            P("expert", "dp", None, None, None),
            P(),
            P(),
            P("expert", None, "dp"),
            P("expert", None, "dp"),
            P(None, "expert", None),
            P(None, "expert", None),
            P(None, "expert", None),
        ),
        out_specs=P(None, "expert", "dp"),
        check_vma=False,
    )
```

```python
import functools
import math

import jax
import jax.numpy as jnp
from jax import lax
from jax.experimental import pallas as pl
from jax.experimental.pallas import tpu as pltpu
from jax.sharding import PartitionSpec as P

learning_rate = 0.03
quant_limit = 448.0
epsilon_value = 1e-06

SIDE = 4
CORES = 2
BLK = 128
EXTRA = 32
TURNS = (0, 1, 3, 2)
ANY = pl.ANY
VMEM = pltpu.VMEM
SMEM = pltpu.SMEM


def vmem():
    return pl.BlockSpec(memory_space=VMEM)


def smem():
    return pl.BlockSpec(memory_space=SMEM)


def shifted(stage, shift):
    pairs = []
    for x in range(SIDE):
        for y in range(SIDE):
            here = (x * SIDE + y) * CORES
            along_x = ((x + shift) % SIDE * SIDE + y) * CORES
            along_y = (x * SIDE + (y + shift) % SIDE) * CORES
            first, second = (along_y, along_x) if stage == 0 else (along_x, along_y)
            pairs += [(here, first), (here + 1, second + 1)]
    return pairs


def core_swap():
    return [(i, i ^ 1) for i in range(SIDE * SIDE * CORES)]


def both_cores():
    return [[CORES * i, CORES * i + 1] for i in range(SIDE * SIDE)]


def same_core():
    return [[2 * i + core for i in range(SIDE * SIDE)] for core in range(CORES)]


def select_kernel(changed_ref, hidden_hbm, cotangent_hbm, out_ref, hidden_ref, cotangent_ref, sems):
    me = lax.axis_index("expert")
    groups, per_group = out_ref.shape[0], out_ref.shape[1]
    first = pltpu.make_async_copy(hidden_hbm, hidden_ref, sems.at[0])
    second = pltpu.make_async_copy(cotangent_hbm, cotangent_ref, sems.at[1])
    first.start()
    second.start()
    first.wait()
    second.wait()
    for g in range(groups):
        for c in range(per_group):
            k = changed_ref[g, c, me]
            e = k >> 4
            r = (k >> 1) & 7
            b = (k & 1) + 2 * g
            out_ref[g, c, 0] = hidden_ref[e, :, pl.ds(pl.multiple_of(r * BLK, BLK), BLK)]
            out_ref[g, c, 1] = cotangent_ref[e, :, pl.ds(pl.multiple_of(b * BLK, BLK), BLK)]


def chunk_kernel(slot_ref, token_hbm, route_hbm, gate_hbm, out_ref, token_ref, route_ref, gate_ref, sems):
    pairs = ((route_hbm, route_ref), (gate_hbm, gate_ref), (token_hbm, token_ref))
    copies = [pltpu.make_async_copy(a, b, sems.at[n]) for n, (a, b) in enumerate(pairs)]
    for copy in copies:
        copy.start()
    for copy in copies:
        copy.wait()
    steps, per_step, width = token_ref.shape
    tokens = steps * per_step
    blocks = width // BLK
    route = jnp.concatenate([route_ref[s] for s in range(steps)], axis=1)
    place = jnp.zeros_like(route)
    for e in range(slot_ref.shape[0]):
        place = jnp.where(route == e, slot_ref[e], place)
    gate = jnp.concatenate([gate_ref[s] for s in range(steps)], axis=1)
    high = gate.astype(jnp.bfloat16).astype(jnp.float32)
    low = (gate - high).astype(jnp.bfloat16).astype(jnp.float32)
    extra = jnp.concatenate([place.astype(jnp.float32), high, low, jnp.zeros_like(low)], axis=0)
    extra = extra.astype(jnp.bfloat16)
    for r in range(blocks):
        tile = token_ref[:, :, r * BLK : (r + 1) * BLK].reshape(tokens, BLK)
        out_ref[r * BLK : (r + 1) * BLK, :] = tile
    out_ref[blocks * BLK :, :] = extra


def gate_columns(x_ref, places):
    base = x_ref.shape[1] - EXTRA
    columns = []
    for q in range(x_ref.shape[0]):
        extra = x_ref[q, base : base + EXTRA, :].astype(jnp.float32)
        place = extra[0:8]
        gate = extra[8:16] + extra[16:24]
        rows = [
            jnp.sum(jnp.where(place == p.astype(jnp.float32), gate, 0.0), axis=0, keepdims=True)
            for p in places
        ]
        rows.append(jnp.zeros((16 - len(places), BLK), jnp.float32))
        columns.append(jnp.transpose(jnp.concatenate(rows, axis=0)))
    return jnp.concatenate(columns, axis=0)


def chip_blocks(changed_ref, slot_ref, exp_dev):
    me, g = lax.axis_index("expert"), lax.axis_index("dp")
    learners = [me // CORES * CORES + c // 2 for c in range(4)]
    codes = [changed_ref[g, c % 2, learners[c]] for c in range(4)]
    return codes, [slot_ref[j * exp_dev + (k >> 4)] for j, k in zip(learners, codes)]


def kept_scales(changed_ref, slot_ref, scale_ref, kept, exp_dev):
    me, g = lax.axis_index("expert"), lax.axis_index("dp")
    chip = me // CORES
    held, per_expert = scale_ref.shape
    for s in range(held):
        for n in range(per_expert):
            kept[s, n] = scale_ref[s, n]
    for j in range(changed_ref.shape[2]):
        for c in range(changed_ref.shape[1]):
            k = changed_ref[g, c, j]
            place = slot_ref[j * exp_dev + (k >> 4)]

            @pl.when(place // held == chip)
            def _():
                kept[place % held, k & 15] = 0.0


def add_lines(changed_ref, slot_ref, exp_dev, lines, weight_of, sum_ref, picked_ref):
    me = lax.axis_index("expert")
    held = CORES * exp_dev
    codes, block_places = chip_blocks(changed_ref, slot_ref, exp_dev)
    places = [me * exp_dev + e for e in range(exp_dev)]
    places += [(me ^ 1) * exp_dev + e for e in range(exp_dev)]
    columns = jnp.concatenate([gate_columns(x, places + block_places) for x in lines], axis=0)
    rows = SIDE * BLK
    blocks = (lines[0].shape[1] - EXTRA) // BLK

    def tiles(at):
        return jnp.concatenate([x[:, at, :].reshape(rows, BLK) for x in lines], axis=0)

    x = jnp.concatenate([tiles(pl.ds(r * BLK, BLK)) for r in range(blocks)], axis=1)
    value = None
    for e in range(held):
        part = jnp.dot(x, weight_of(e), preferred_element_type=jnp.float32)
        part = part * columns[:, e : e + 1]
        value = part if value is None else value + part
    sum_ref[...] = value.astype(sum_ref.dtype)
    for c in range(4):
        r = (codes[c] >> 1) & 7
        tile = tiles(pl.ds(pl.multiple_of(r * BLK, BLK), BLK))
        gated = tile.astype(jnp.float32) * columns[:, held + c : held + c + 1]
        picked_ref[:, c * BLK : (c + 1) * BLK] = gated.astype(jnp.bfloat16)


def first_kernel(
    changed_ref, slot_ref, scale_ref, own_ref, other_ref, x0, x1, weight_ref, sum_ref, picked_ref, kept
):
    me = lax.axis_index("expert")
    exp_dev = own_ref.shape[0]
    kept_scales(changed_ref, slot_ref, scale_ref, kept, exp_dev)

    def weight_of(e):
        ref = own_ref if e < exp_dev else other_ref
        place = (me + e // exp_dev) % CORES * exp_dev + e % exp_dev
        for n in range(scale_ref.shape[1]):
            rows, columns = pl.ds(n // 2 * BLK, BLK), pl.ds(n % 2 * BLK, BLK)
            scaled = ref[e % exp_dev, rows, columns].astype(jnp.float32) * kept[place, n]
            weight_ref[e, rows, columns] = scaled.astype(jnp.bfloat16)
        return weight_ref[e]

    add_lines(changed_ref, slot_ref, exp_dev, (x0, x1), weight_of, sum_ref, picked_ref)


def second_kernel(changed_ref, slot_ref, weight_ref, x2, x3, sum_ref, picked_ref):
    exp_dev = weight_ref.shape[0] // CORES
    weight_of = lambda e: weight_ref[e]
    add_lines(changed_ref, slot_ref, exp_dev, (x2, x3), weight_of, sum_ref, picked_ref)


def refresh_kernel(recv_ref, master_ref, out_ref, *, step_size):
    groups, per_group = recv_ref.shape[0], recv_ref.shape[1]
    rows = groups * recv_ref.shape[3]
    for c in range(per_group):
        left = recv_ref[:, c, 0].reshape(rows, BLK)
        right = recv_ref[:, c, 1].reshape(rows, BLK)
        gradient = lax.dot_general(
            left, right, (((0,), (0,)), ((), ())), preferred_element_type=jnp.float32
        )
        updated = master_ref[c] - step_size * gradient
        peak = jnp.max(jnp.max(jnp.abs(updated), axis=0, keepdims=True), axis=1, keepdims=True)
        scale = ((peak + epsilon_value) / quant_limit).astype(jnp.bfloat16)
        scale = jnp.broadcast_to(scale.astype(jnp.float32), (16, BLK))
        out_ref[c, 0:BLK, :] = (updated / scale[0:1, :]).astype(jnp.bfloat16)
        out_ref[c, BLK : BLK + 16, :] = scale.astype(jnp.bfloat16)


def last_kernel(changed_ref, slot_ref, block_ref, s0, s1, p0, p1, out_ref, spread):
    me = lax.axis_index("expert")
    chip, core = me // CORES, me % CORES
    x, y = chip // SIDE, chip % SIDE
    codes, _ = chip_blocks(changed_ref, slot_ref, 4)
    spread[...] = jnp.zeros(spread.shape, spread.dtype)
    for c in range(4):
        scale = block_ref[c, BLK : BLK + 16, :].astype(jnp.float32)[0:1]
        at = pl.ds(pl.multiple_of((codes[c] & 1) * BLK, BLK), BLK)
        value = block_ref[c, 0:BLK, :].astype(jnp.float32) * scale
        spread[c * BLK : (c + 1) * BLK, at] = value.astype(jnp.bfloat16)
    for half, (sum_ref, picked_ref) in enumerate(((s0, p0), (s1, p1))):
        delta = jnp.dot(picked_ref[...], spread[...], preferred_element_type=jnp.float32)
        total = (sum_ref[...].astype(jnp.float32) + delta).astype(jnp.bfloat16)
        for n in range(2 * SIDE):
            second, first = TURNS[2 * half + n // SIDE], TURNS[n % SIDE]
            x_back = jnp.where(core == 0, second, first)
            y_back = jnp.where(core == 0, first, second)
            to = (x + SIDE - x_back) % SIDE * SIDE + (y + SIDE - y_back) % SIDE
            out_ref[to] = total[n * BLK : (n + 1) * BLK, :]


def shards(
    learn_hidden,
    learn_cotangent,
    master_blocks,
    changed,
    rollout_slot,
    rollout_weight,
    rollout_scale,
    decode_hidden,
    decode_routes,
    decode_gates,
):
    dp_count = lax.axis_size("dp")
    exp_dev, learn_rows, width_ff = learn_hidden.shape[1:]
    width_local = rollout_weight.shape[2]
    per_group = master_blocks.shape[2]
    tokens = decode_hidden.shape[0] * decode_hidden.shape[1]
    rows = SIDE * tokens
    limit = pltpu.CompilerParams(vmem_limit_bytes=32 * 1024 * 1024)
    whole = pltpu.CompilerParams(vmem_limit_bytes=60 * 1024 * 1024)
    table = jnp.transpose(changed, (1, 2, 0))

    token_args = (
        decode_hidden,
        jnp.transpose(decode_routes, (0, 2, 1)),
        jnp.transpose(decode_gates, (0, 2, 1)),
    )
    chunk = pl.pallas_call(
        chunk_kernel,
        out_shape=jax.ShapeDtypeStruct((width_ff + EXTRA, BLK), jnp.bfloat16),
        in_specs=[smem()] + [pl.BlockSpec(memory_space=ANY)] * 3,
        out_specs=vmem(),
        scratch_shapes=[pltpu.VMEM(a.shape, a.dtype) for a in token_args]
        + [pltpu.SemaphoreType.DMA((3,))],
        compiler_params=whole,
    )(rollout_slot, *token_args)
    chunk, learn_hidden, learn_cotangent, rollout_weight = lax.optimization_barrier(
        (chunk, learn_hidden, learn_cotangent, rollout_weight)
    )
    line = jnp.stack(
        [chunk] + [lax.ppermute(chunk, "expert", shifted(0, turn)) for turn in TURNS[1:]]
    )

    tiles = pl.pallas_call(
        select_kernel,
        out_shape=jax.ShapeDtypeStruct((dp_count, per_group, 2, learn_rows, BLK), jnp.bfloat16),
        in_specs=[smem()] + [pl.BlockSpec(memory_space=ANY)] * 2,
        out_specs=vmem(),
        scratch_shapes=[
            pltpu.VMEM(learn_hidden.shape[1:], jnp.bfloat16),
            pltpu.VMEM(learn_cotangent.shape[1:], jnp.bfloat16),
            pltpu.SemaphoreType.DMA((2,)),
        ],
        compiler_params=whole,
    )(table, learn_hidden[0], learn_cotangent[0])
    line, tiles = lax.optimization_barrier((line, tiles))
    received = lax.all_to_all(tiles, "dp", 0, 0, tiled=True)

    right = lax.ppermute(line, "expert", shifted(1, 1))
    line, right = lax.optimization_barrier((line, right))
    far = lax.ppermute(right, "expert", shifted(1, 1))
    left = lax.ppermute(line, "expert", shifted(1, -1))

    other_weight = lax.ppermute(rollout_weight, "expert", core_swap())
    line, rollout_scale = lax.optimization_barrier((line, rollout_scale))
    scales = lax.all_gather(
        rollout_scale, "expert", axis_index_groups=both_cores(), tiled=True
    )
    scales = scales.astype(jnp.float32).reshape(CORES * exp_dev, -1)

    cost = pl.CostEstimate(
        flops=2 * 2 * rows * width_ff * width_local * 8,
        bytes_accessed=12 * 1024 * 1024,
        transcendentals=0,
    )
    pair_out = (
        jax.ShapeDtypeStruct((2 * rows, width_local), jnp.bfloat16),
        jax.ShapeDtypeStruct((2 * rows, 4 * BLK), jnp.bfloat16),
    )
    held = CORES * exp_dev
    weights, sum_first, picked_first = pl.pallas_call(
        first_kernel,
        out_shape=(jax.ShapeDtypeStruct((held,) + rollout_weight.shape[1:], jnp.bfloat16),)
        + pair_out,
        in_specs=[smem()] * 3 + [vmem()] * 4,
        out_specs=(vmem(),) * 3,
        scratch_shapes=[pltpu.SMEM((held, 16), jnp.float32)],
        compiler_params=limit,
        cost_estimate=cost,
    )(table, rollout_slot, scales, rollout_weight, other_weight, line, right)
    left, far, sum_first = lax.optimization_barrier((left, far, sum_first))
    sum_second, picked_second = pl.pallas_call(
        second_kernel,
        out_shape=pair_out,
        in_specs=[smem()] * 2 + [vmem()] * 3,
        out_specs=(vmem(),) * 2,
        compiler_params=limit,
        cost_estimate=cost,
    )(table, rollout_slot, weights, left, far)
    received, sum_second = lax.optimization_barrier((received, sum_second))

    step_size = learning_rate / math.sqrt(dp_count * learn_rows)
    own_block = pl.pallas_call(
        functools.partial(refresh_kernel, step_size=step_size),
        out_shape=jax.ShapeDtypeStruct((per_group, BLK + 16, BLK), jnp.bfloat16),
        in_specs=[vmem(), vmem()],
        out_specs=vmem(),
        compiler_params=limit,
    )(received, master_blocks[0, 0])
    blocks = lax.all_gather(own_block, "expert", axis_index_groups=both_cores(), tiled=True)

    outgoing = pl.pallas_call(
        last_kernel,
        out_shape=jax.ShapeDtypeStruct((SIDE * SIDE, tokens, width_local), jnp.bfloat16),
        in_specs=[smem()] * 2 + [vmem()] * 5,
        out_specs=vmem(),
        scratch_shapes=[pltpu.VMEM((4 * BLK, width_local), jnp.bfloat16)],
        compiler_params=limit,
    )(table, rollout_slot, blocks, sum_first, sum_second, picked_first, picked_second)

    returned = lax.all_to_all(
        outgoing, "expert", 0, 0, axis_index_groups=same_core(), tiled=True
    )
    result = jnp.sum(returned.astype(jnp.float32), axis=0).astype(jnp.bfloat16)
    return result.reshape(decode_hidden.shape[0], decode_hidden.shape[1], width_local)


def solution(mesh):
    return jax.shard_map(
        shards,
        mesh=mesh,
        in_specs=(
            P("dp", "expert", None, None),
            P("dp", "expert", None, None),
            P("expert", "dp", None, None, None),
            P(),
            P(),
            P("expert", None, "dp"),
            P("expert", None, "dp"),
            P(None, "expert", None),
            P(None, "expert", None),
            P(None, "expert", None),
        ),
        out_specs=P(None, "expert", "dp"),
        check_vma=False,
    )
```

```python
import functools
import math

import jax
import jax.numpy as jnp
from jax import lax
from jax.experimental import pallas as pl
from jax.experimental.pallas import tpu as pltpu
from jax.sharding import PartitionSpec as P

learning_rate = 0.03
quant_limit = 448.0
epsilon_value = 1e-06

SIDE = 4
CORES = 2
BLK = 128
EXTRA = 32
TURNS = (0, 1, 3, 2)
ANY = pl.ANY
VMEM = pltpu.VMEM
SMEM = pltpu.SMEM


def vmem():
    return pl.BlockSpec(memory_space=VMEM)


def smem():
    return pl.BlockSpec(memory_space=SMEM)


def shifted(stage, shift):
    pairs = []
    for x in range(SIDE):
        for y in range(SIDE):
            here = (x * SIDE + y) * CORES
            along_x = ((x + shift) % SIDE * SIDE + y) * CORES
            along_y = (x * SIDE + (y + shift) % SIDE) * CORES
            first, second = (along_y, along_x) if stage == 0 else (along_x, along_y)
            pairs += [(here, first), (here + 1, second + 1)]
    return pairs


def lines():
    along_y = [[(x * SIDE + y) * CORES for y in range(SIDE)] for x in range(SIDE)]
    along_x = [[(x * SIDE + y) * CORES + 1 for x in range(SIDE)] for y in range(SIDE)]
    return along_y + along_x


def core_swap():
    return [(i, i ^ 1) for i in range(SIDE * SIDE * CORES)]


def both_cores():
    return [[CORES * i, CORES * i + 1] for i in range(SIDE * SIDE)]


def same_core():
    return [[2 * i + core for i in range(SIDE * SIDE)] for core in range(CORES)]


def select_kernel(changed_ref, hidden_hbm, cotangent_hbm, out_ref, hidden_ref, cotangent_ref, sems):
    me = lax.axis_index("expert")
    groups, per_group = out_ref.shape[0], out_ref.shape[1]
    first = pltpu.make_async_copy(hidden_hbm, hidden_ref, sems.at[0])
    second = pltpu.make_async_copy(cotangent_hbm, cotangent_ref, sems.at[1])
    first.start()
    second.start()
    first.wait()
    second.wait()
    for g in range(groups):
        for c in range(per_group):
            k = changed_ref[g, c, me]
            e = k >> 4
            r = (k >> 1) & 7
            b = (k & 1) + 2 * g
            out_ref[g, c, 0] = hidden_ref[e, :, pl.ds(pl.multiple_of(r * BLK, BLK), BLK)]
            out_ref[g, c, 1] = cotangent_ref[e, :, pl.ds(pl.multiple_of(b * BLK, BLK), BLK)]


def chunk_kernel(slot_ref, token_hbm, route_hbm, gate_hbm, out_ref, token_ref, route_ref, gate_ref, sems):
    pairs = ((route_hbm, route_ref), (gate_hbm, gate_ref), (token_hbm, token_ref))
    copies = [pltpu.make_async_copy(a, b, sems.at[n]) for n, (a, b) in enumerate(pairs)]
    for copy in copies:
        copy.start()
    for copy in copies:
        copy.wait()
    steps, per_step, width = token_ref.shape
    tokens = steps * per_step
    blocks = width // BLK
    route = jnp.concatenate([route_ref[s] for s in range(steps)], axis=1)
    place = jnp.zeros_like(route)
    for e in range(slot_ref.shape[0]):
        place = jnp.where(route == e, slot_ref[e], place)
    gate = jnp.concatenate([gate_ref[s] for s in range(steps)], axis=1)
    high = gate.astype(jnp.bfloat16).astype(jnp.float32)
    low = (gate - high).astype(jnp.bfloat16).astype(jnp.float32)
    extra = jnp.concatenate([place.astype(jnp.float32), high, low, jnp.zeros_like(low)], axis=0)
    extra = extra.astype(jnp.bfloat16)
    for copy in range(out_ref.shape[0]):
        for r in range(blocks):
            tile = token_ref[:, :, r * BLK : (r + 1) * BLK].reshape(tokens, BLK)
            out_ref[copy, r * BLK : (r + 1) * BLK, :] = tile
        out_ref[copy, blocks * BLK :, :] = extra


def gate_columns(x_ref, places):
    base = x_ref.shape[1] - EXTRA
    columns = []
    for q in range(x_ref.shape[0]):
        extra = x_ref[q, base : base + EXTRA, :].astype(jnp.float32)
        place = extra[0:8]
        gate = extra[8:16] + extra[16:24]
        rows = [
            jnp.sum(jnp.where(place == p.astype(jnp.float32), gate, 0.0), axis=0, keepdims=True)
            for p in places
        ]
        rows.append(jnp.zeros((16 - len(places), BLK), jnp.float32))
        columns.append(jnp.transpose(jnp.concatenate(rows, axis=0)))
    return jnp.concatenate(columns, axis=0)


def chip_blocks(changed_ref, slot_ref, exp_dev):
    me, g = lax.axis_index("expert"), lax.axis_index("dp")
    learners = [me // CORES * CORES + c // 2 for c in range(4)]
    codes = [changed_ref[g, c % 2, learners[c]] for c in range(4)]
    return codes, [slot_ref[j * exp_dev + (k >> 4)] for j, k in zip(learners, codes)]


def kept_scales(changed_ref, slot_ref, scale_ref, kept, exp_dev):
    me, g = lax.axis_index("expert"), lax.axis_index("dp")
    chip = me // CORES
    held, per_expert = scale_ref.shape
    for s in range(held):
        for n in range(per_expert):
            kept[s, n] = scale_ref[s, n]
    for j in range(changed_ref.shape[2]):
        for c in range(changed_ref.shape[1]):
            k = changed_ref[g, c, j]
            place = slot_ref[j * exp_dev + (k >> 4)]
            row = jnp.where(place >> 3 == chip, place & 7, held)
            kept[row, k & 15] = 0.0


def add_lines(changed_ref, slot_ref, exp_dev, lines, weight_of, sum_ref, picked_ref):
    me = lax.axis_index("expert")
    held = CORES * exp_dev
    codes, block_places = chip_blocks(changed_ref, slot_ref, exp_dev)
    places = [me * exp_dev + e for e in range(exp_dev)]
    places += [(me ^ 1) * exp_dev + e for e in range(exp_dev)]
    columns = jnp.concatenate([gate_columns(x, places + block_places) for x in lines], axis=0)
    rows = SIDE * BLK
    blocks = (lines[0].shape[1] - EXTRA) // BLK

    def tiles(at):
        return jnp.concatenate([x[:, at, :].reshape(rows, BLK) for x in lines], axis=0)

    x = jnp.concatenate([tiles(pl.ds(r * BLK, BLK)) for r in range(blocks)], axis=1)
    value = None
    for e in range(held):
        part = jnp.dot(x, weight_of(e), preferred_element_type=jnp.float32)
        part = part * columns[:, e : e + 1]
        value = part if value is None else value + part
    sum_ref[...] = value.astype(sum_ref.dtype)
    for c in range(4):
        r = (codes[c] >> 1) & 7
        tile = tiles(pl.ds(pl.multiple_of(r * BLK, BLK), BLK))
        gated = tile.astype(jnp.float32) * columns[:, held + c : held + c + 1]
        picked_ref[:, c * BLK : (c + 1) * BLK] = gated.astype(jnp.bfloat16)


def first_kernel(
    changed_ref, slot_ref, scale_ref, own_ref, other_ref, x0, x1, weight_ref, sum_ref, picked_ref, kept
):
    me = lax.axis_index("expert")
    exp_dev = own_ref.shape[0]
    kept_scales(changed_ref, slot_ref, scale_ref, kept, exp_dev)

    def weight_of(e):
        ref = own_ref if e < exp_dev else other_ref
        place = (me + e // exp_dev) % CORES * exp_dev + e % exp_dev
        for n in range(scale_ref.shape[1]):
            rows, columns = pl.ds(n // 2 * BLK, BLK), pl.ds(n % 2 * BLK, BLK)
            scaled = ref[e % exp_dev, rows, columns].astype(jnp.float32) * kept[place, n]
            weight_ref[e, rows, columns] = scaled.astype(jnp.bfloat16)
        return weight_ref[e]

    add_lines(changed_ref, slot_ref, exp_dev, (x0, x1), weight_of, sum_ref, picked_ref)


def line_kernel(changed_ref, slot_ref, weight_ref, x_ref, sum_ref, picked_ref):
    exp_dev = weight_ref.shape[0] // CORES
    weight_of = lambda e: weight_ref[e]
    add_lines(changed_ref, slot_ref, exp_dev, (x_ref,), weight_of, sum_ref, picked_ref)


def refresh_kernel(recv_ref, master_ref, out_ref, *, step_size):
    groups, per_group = recv_ref.shape[0], recv_ref.shape[1]
    rows = groups * recv_ref.shape[3]
    for c in range(per_group):
        left = recv_ref[:, c, 0].reshape(rows, BLK)
        right = recv_ref[:, c, 1].reshape(rows, BLK)
        gradient = lax.dot_general(
            left, right, (((0,), (0,)), ((), ())), preferred_element_type=jnp.float32
        )
        updated = master_ref[c] - step_size * gradient
        peak = jnp.max(jnp.max(jnp.abs(updated), axis=0, keepdims=True), axis=1, keepdims=True)
        scale = ((peak + epsilon_value) / quant_limit).astype(jnp.bfloat16)
        scale = jnp.broadcast_to(scale.astype(jnp.float32), (16, BLK))
        out_ref[c, 0:BLK, :] = (updated / scale[0:1, :]).astype(jnp.bfloat16)
        out_ref[c, BLK : BLK + 16, :] = scale.astype(jnp.bfloat16)


def last_kernel(changed_ref, slot_ref, block_ref, s0, s1, s2, p0, p1, p2, out_ref, spread):
    me = lax.axis_index("expert")
    chip, core = me // CORES, me % CORES
    x, y = chip // SIDE, chip % SIDE
    codes, _ = chip_blocks(changed_ref, slot_ref, 4)
    spread[...] = jnp.zeros(spread.shape, spread.dtype)
    for c in range(4):
        scale = block_ref[c, BLK : BLK + 16, :].astype(jnp.float32)[0:1]
        at = pl.ds(pl.multiple_of((codes[c] & 1) * BLK, BLK), BLK)
        value = block_ref[c, 0:BLK, :].astype(jnp.float32) * scale
        spread[c * BLK : (c + 1) * BLK, at] = value.astype(jnp.bfloat16)
    number = 0
    for sum_ref, picked_ref in ((s0, p0), (s1, p1), (s2, p2)):
        delta = jnp.dot(picked_ref[...], spread[...], preferred_element_type=jnp.float32)
        total = (sum_ref[...].astype(jnp.float32) + delta).astype(jnp.bfloat16)
        for n in range(sum_ref.shape[0] // BLK):
            second, first = TURNS[number // SIDE], number % SIDE
            number += 1
            along_y = (x + SIDE - second) % SIDE * SIDE + first
            along_x = first * SIDE + (y + SIDE - second) % SIDE
            to = jnp.where(core == 0, along_y, along_x)
            out_ref[to] = total[n * BLK : (n + 1) * BLK, :]


def shards(
    learn_hidden,
    learn_cotangent,
    master_blocks,
    changed,
    rollout_slot,
    rollout_weight,
    rollout_scale,
    decode_hidden,
    decode_routes,
    decode_gates,
):
    dp_count = lax.axis_size("dp")
    exp_dev, learn_rows, width_ff = learn_hidden.shape[1:]
    width_local = rollout_weight.shape[2]
    per_group = master_blocks.shape[2]
    tokens = decode_hidden.shape[0] * decode_hidden.shape[1]
    rows = SIDE * tokens
    limit = pltpu.CompilerParams(vmem_limit_bytes=32 * 1024 * 1024)
    whole = pltpu.CompilerParams(vmem_limit_bytes=60 * 1024 * 1024)
    table = jnp.transpose(changed, (1, 2, 0))

    token_args = (
        decode_hidden,
        jnp.transpose(decode_routes, (0, 2, 1)),
        jnp.transpose(decode_gates, (0, 2, 1)),
    )
    chunk = pl.pallas_call(
        chunk_kernel,
        out_shape=jax.ShapeDtypeStruct((SIDE, width_ff + EXTRA, BLK), jnp.bfloat16),
        in_specs=[smem()] + [pl.BlockSpec(memory_space=ANY)] * 3,
        out_specs=vmem(),
        scratch_shapes=[pltpu.VMEM(a.shape, a.dtype) for a in token_args]
        + [pltpu.SemaphoreType.DMA((3,))],
        compiler_params=whole,
    )(rollout_slot, *token_args)
    chunk, learn_hidden, learn_cotangent, rollout_weight = lax.optimization_barrier(
        (chunk, learn_hidden, learn_cotangent, rollout_weight)
    )
    line = lax.all_to_all(chunk, "expert", 0, 0, axis_index_groups=lines(), tiled=True)

    tiles = pl.pallas_call(
        select_kernel,
        out_shape=jax.ShapeDtypeStruct((dp_count, per_group, 2, learn_rows, BLK), jnp.bfloat16),
        in_specs=[smem()] + [pl.BlockSpec(memory_space=ANY)] * 2,
        out_specs=vmem(),
        scratch_shapes=[
            pltpu.VMEM(learn_hidden.shape[1:], jnp.bfloat16),
            pltpu.VMEM(learn_cotangent.shape[1:], jnp.bfloat16),
            pltpu.SemaphoreType.DMA((2,)),
        ],
        compiler_params=whole,
    )(table, learn_hidden[0], learn_cotangent[0])
    line, tiles = lax.optimization_barrier((line, tiles))
    received = lax.all_to_all(tiles, "dp", 0, 0, tiled=True)

    right = lax.ppermute(line, "expert", shifted(1, 1))
    line, right = lax.optimization_barrier((line, right))
    far = lax.ppermute(right, "expert", shifted(1, 1))
    left = lax.ppermute(line, "expert", shifted(1, -1))

    other_weight = lax.ppermute(rollout_weight, "expert", core_swap())
    line, rollout_scale = lax.optimization_barrier((line, rollout_scale))
    scales = lax.all_gather(
        rollout_scale, "expert", axis_index_groups=both_cores(), tiled=True
    )
    scales = scales.astype(jnp.float32).reshape(CORES * exp_dev, -1)

    def cost(lines):
        return pl.CostEstimate(
            flops=lines * 2 * rows * width_ff * width_local * 8,
            bytes_accessed=lines * 6 * 1024 * 1024,
            transcendentals=0,
        )

    def sums_of(lines):
        return (
            jax.ShapeDtypeStruct((lines * rows, width_local), jnp.bfloat16),
            jax.ShapeDtypeStruct((lines * rows, 4 * BLK), jnp.bfloat16),
        )

    held = CORES * exp_dev
    weights, sum_first, picked_first = pl.pallas_call(
        first_kernel,
        out_shape=(jax.ShapeDtypeStruct((held,) + rollout_weight.shape[1:], jnp.bfloat16),)
        + sums_of(2),
        in_specs=[smem()] * 3 + [vmem()] * 4,
        out_specs=(vmem(),) * 3,
        scratch_shapes=[pltpu.SMEM((held + 1, 16), jnp.float32)],
        compiler_params=limit,
        cost_estimate=cost(2),
    )(table, rollout_slot, scales, rollout_weight, other_weight, line, right)

    def add_line(piece):
        return pl.pallas_call(
            line_kernel,
            out_shape=sums_of(1),
            in_specs=[smem()] * 2 + [vmem()] * 2,
            out_specs=(vmem(),) * 2,
            compiler_params=limit,
            cost_estimate=cost(1),
        )(table, rollout_slot, weights, piece)

    left, sum_first = lax.optimization_barrier((left, sum_first))
    sum_left, picked_left = add_line(left)
    far, sum_left = lax.optimization_barrier((far, sum_left))
    sum_far, picked_far = add_line(far)
    received, sum_far = lax.optimization_barrier((received, sum_far))

    step_size = learning_rate / math.sqrt(dp_count * learn_rows)
    own_block = pl.pallas_call(
        functools.partial(refresh_kernel, step_size=step_size),
        out_shape=jax.ShapeDtypeStruct((per_group, BLK + 16, BLK), jnp.bfloat16),
        in_specs=[vmem(), vmem()],
        out_specs=vmem(),
        compiler_params=limit,
    )(received, master_blocks[0, 0])
    blocks = lax.all_gather(own_block, "expert", axis_index_groups=both_cores(), tiled=True)

    outgoing = pl.pallas_call(
        last_kernel,
        out_shape=jax.ShapeDtypeStruct((SIDE * SIDE, tokens, width_local), jnp.bfloat16),
        in_specs=[smem()] * 2 + [vmem()] * 7,
        out_specs=vmem(),
        scratch_shapes=[pltpu.VMEM((4 * BLK, width_local), jnp.bfloat16)],
        compiler_params=limit,
    )(
        table, rollout_slot, blocks,
        sum_first, sum_left, sum_far, picked_first, picked_left, picked_far,
    )

    returned = lax.all_to_all(
        outgoing, "expert", 0, 0, axis_index_groups=same_core(), tiled=True
    )
    result = jnp.sum(returned.astype(jnp.float32), axis=0).astype(jnp.bfloat16)
    return result.reshape(decode_hidden.shape[0], decode_hidden.shape[1], width_local)


def solution(mesh):
    return jax.shard_map(
        shards,
        mesh=mesh,
        in_specs=(
            P("dp", "expert", None, None),
            P("dp", "expert", None, None),
            P("expert", "dp", None, None, None),
            P(),
            P(),
            P("expert", None, "dp"),
            P("expert", None, "dp"),
            P(None, "expert", None),
            P(None, "expert", None),
            P(None, "expert", None),
        ),
        out_specs=P(None, "expert", "dp"),
        check_vma=False,
    )
```

```python
import functools
import math

import jax
import jax.numpy as jnp
from jax import lax
from jax.experimental import pallas as pl
from jax.experimental.pallas import tpu as pltpu
from jax.sharding import PartitionSpec as P

learning_rate = 0.03
quant_limit = 448.0
epsilon_value = 1e-06

SIDE = 4
CORES = 2
BLK = 128
EXTRA = 32
TURNS = (0, 1, 3, 2)
ANY = pl.ANY
VMEM = pltpu.VMEM
SMEM = pltpu.SMEM


def vmem():
    return pl.BlockSpec(memory_space=VMEM)


def smem():
    return pl.BlockSpec(memory_space=SMEM)


def shifted(stage, shift):
    pairs = []
    for x in range(SIDE):
        for y in range(SIDE):
            here = (x * SIDE + y) * CORES
            along_x = ((x + shift) % SIDE * SIDE + y) * CORES
            along_y = (x * SIDE + (y + shift) % SIDE) * CORES
            first, second = (along_y, along_x) if stage == 0 else (along_x, along_y)
            pairs += [(here, first), (here + 1, second + 1)]
    return pairs


def lines():
    along_y = [[(x * SIDE + y) * CORES for y in range(SIDE)] for x in range(SIDE)]
    along_x = [[(x * SIDE + y) * CORES + 1 for x in range(SIDE)] for y in range(SIDE)]
    return along_y + along_x


def core_swap():
    return [(i, i ^ 1) for i in range(SIDE * SIDE * CORES)]


def both_cores():
    return [[CORES * i, CORES * i + 1] for i in range(SIDE * SIDE)]


def same_core():
    return [[2 * i + core for i in range(SIDE * SIDE)] for core in range(CORES)]


def select_kernel(changed_ref, hidden_hbm, cotangent_hbm, out_ref, hidden_ref, cotangent_ref, sems):
    me = lax.axis_index("expert")
    groups, per_group = out_ref.shape[0], out_ref.shape[1]
    first = pltpu.make_async_copy(hidden_hbm, hidden_ref, sems.at[0])
    second = pltpu.make_async_copy(cotangent_hbm, cotangent_ref, sems.at[1])
    first.start()
    second.start()
    first.wait()
    second.wait()
    for g in range(groups):
        for c in range(per_group):
            k = changed_ref[g, c, me]
            e = k >> 4
            r = (k >> 1) & 7
            b = (k & 1) + 2 * g
            out_ref[g, c, 0] = hidden_ref[e, :, pl.ds(pl.multiple_of(r * BLK, BLK), BLK)]
            out_ref[g, c, 1] = cotangent_ref[e, :, pl.ds(pl.multiple_of(b * BLK, BLK), BLK)]


def chunk_kernel(slot_ref, token_hbm, route_hbm, gate_hbm, out_ref, token_ref, route_ref, gate_ref, sems):
    pairs = ((route_hbm, route_ref), (gate_hbm, gate_ref), (token_hbm, token_ref))
    copies = [pltpu.make_async_copy(a, b, sems.at[n]) for n, (a, b) in enumerate(pairs)]
    for copy in copies:
        copy.start()
    for copy in copies:
        copy.wait()
    steps, per_step, width = token_ref.shape
    tokens = steps * per_step
    blocks = width // BLK
    route = jnp.concatenate([route_ref[s] for s in range(steps)], axis=1)
    place = jnp.zeros_like(route)
    for e in range(slot_ref.shape[0]):
        place = jnp.where(route == e, slot_ref[e], place)
    gate = jnp.concatenate([gate_ref[s] for s in range(steps)], axis=1)
    high = gate.astype(jnp.bfloat16).astype(jnp.float32)
    low = (gate - high).astype(jnp.bfloat16).astype(jnp.float32)
    extra = jnp.concatenate([place.astype(jnp.float32), high, low, jnp.zeros_like(low)], axis=0)
    extra = extra.astype(jnp.bfloat16)
    for copy in range(out_ref.shape[0]):
        for r in range(blocks):
            tile = token_ref[:, :, r * BLK : (r + 1) * BLK].reshape(tokens, BLK)
            out_ref[copy, r * BLK : (r + 1) * BLK, :] = tile
        out_ref[copy, blocks * BLK :, :] = extra


def gate_columns(x_ref, places):
    base = x_ref.shape[1] - EXTRA
    columns = []
    for q in range(x_ref.shape[0]):
        extra = x_ref[q, base : base + EXTRA, :].astype(jnp.float32)
        place = extra[0:8]
        gate = extra[8:16] + extra[16:24]
        rows = [
            jnp.sum(jnp.where(place == p.astype(jnp.float32), gate, 0.0), axis=0, keepdims=True)
            for p in places
        ]
        rows.append(jnp.zeros((16 - len(places), BLK), jnp.float32))
        columns.append(jnp.transpose(jnp.concatenate(rows, axis=0)))
    return jnp.concatenate(columns, axis=0)


def chip_blocks(changed_ref, slot_ref, exp_dev):
    me, g = lax.axis_index("expert"), lax.axis_index("dp")
    learners = [me // CORES * CORES + c // 2 for c in range(4)]
    codes = [changed_ref[g, c % 2, learners[c]] for c in range(4)]
    return codes, [slot_ref[j * exp_dev + (k >> 4)] for j, k in zip(learners, codes)]


def kept_scales(changed_ref, slot_ref, scale_ref, kept, exp_dev):
    me, g = lax.axis_index("expert"), lax.axis_index("dp")
    chip = me // CORES
    held, per_expert = scale_ref.shape
    for s in range(held):
        for n in range(per_expert):
            kept[s, n] = scale_ref[s, n]
    for j in range(changed_ref.shape[2]):
        for c in range(changed_ref.shape[1]):
            k = changed_ref[g, c, j]
            place = slot_ref[j * exp_dev + (k >> 4)]
            row = jnp.where(place >> 3 == chip, place & 7, held)
            kept[row, k & 15] = 0.0


def add_lines(changed_ref, slot_ref, exp_dev, lines, weight_of, sum_ref, picked_ref):
    me = lax.axis_index("expert")
    held = CORES * exp_dev
    codes, block_places = chip_blocks(changed_ref, slot_ref, exp_dev)
    places = [me * exp_dev + e for e in range(exp_dev)]
    places += [(me ^ 1) * exp_dev + e for e in range(exp_dev)]
    columns = jnp.concatenate([gate_columns(x, places + block_places) for x in lines], axis=0)
    rows = SIDE * BLK
    blocks = (lines[0].shape[1] - EXTRA) // BLK

    def tiles(at):
        return jnp.concatenate([x[:, at, :].reshape(rows, BLK) for x in lines], axis=0)

    x = jnp.concatenate([tiles(pl.ds(r * BLK, BLK)) for r in range(blocks)], axis=1)
    value = None
    for e in range(held):
        part = jnp.dot(x, weight_of(e), preferred_element_type=jnp.float32)
        part = part * columns[:, e : e + 1]
        value = part if value is None else value + part
    sum_ref[...] = value.astype(sum_ref.dtype)
    for c in range(4):
        r = (codes[c] >> 1) & 7
        tile = tiles(pl.ds(pl.multiple_of(r * BLK, BLK), BLK))
        gated = tile.astype(jnp.float32) * columns[:, held + c : held + c + 1]
        picked_ref[:, c * BLK : (c + 1) * BLK] = gated.astype(jnp.bfloat16)


def first_kernel(
    changed_ref, slot_ref, scale_ref, own_ref, other_ref, x0, x1, weight_ref, sum_ref, picked_ref, kept
):
    me = lax.axis_index("expert")
    exp_dev = own_ref.shape[0]
    kept_scales(changed_ref, slot_ref, scale_ref, kept, exp_dev)

    def weight_of(e):
        ref = own_ref if e < exp_dev else other_ref
        place = (me + e // exp_dev) % CORES * exp_dev + e % exp_dev
        for n in range(scale_ref.shape[1]):
            rows, columns = pl.ds(n // 2 * BLK, BLK), pl.ds(n % 2 * BLK, BLK)
            scaled = ref[e % exp_dev, rows, columns].astype(jnp.float32) * kept[place, n]
            weight_ref[e, rows, columns] = scaled.astype(jnp.bfloat16)
        return weight_ref[e]

    add_lines(changed_ref, slot_ref, exp_dev, (x0, x1), weight_of, sum_ref, picked_ref)


def line_kernel(changed_ref, slot_ref, weight_ref, x_ref, sum_ref, picked_ref):
    exp_dev = weight_ref.shape[0] // CORES
    weight_of = lambda e: weight_ref[e]
    add_lines(changed_ref, slot_ref, exp_dev, (x_ref,), weight_of, sum_ref, picked_ref)


def refresh_kernel(recv_ref, master_ref, out_ref, *, step_size):
    groups, per_group = recv_ref.shape[0], recv_ref.shape[1]
    rows = groups * recv_ref.shape[3]
    for c in range(per_group):
        left = recv_ref[:, c, 0].reshape(rows, BLK)
        right = recv_ref[:, c, 1].reshape(rows, BLK)
        gradient = lax.dot_general(
            left, right, (((0,), (0,)), ((), ())), preferred_element_type=jnp.float32
        )
        updated = master_ref[c] - step_size * gradient
        peak = jnp.max(jnp.max(jnp.abs(updated), axis=0, keepdims=True), axis=1, keepdims=True)
        scale = ((peak + epsilon_value) / quant_limit).astype(jnp.bfloat16)
        scale = jnp.broadcast_to(scale.astype(jnp.float32), (16, BLK))
        out_ref[c, 0:BLK, :] = (updated / scale[0:1, :]).astype(jnp.bfloat16)
        out_ref[c, BLK : BLK + 16, :] = scale.astype(jnp.bfloat16)


def last_kernel(changed_ref, slot_ref, block_ref, s0, s1, s2, p0, p1, p2, out_ref, spread):
    me = lax.axis_index("expert")
    chip, core = me // CORES, me % CORES
    x, y = chip // SIDE, chip % SIDE
    codes, _ = chip_blocks(changed_ref, slot_ref, 4)
    spread[...] = jnp.zeros(spread.shape, spread.dtype)
    for c in range(4):
        scale = block_ref[c, BLK : BLK + 16, :].astype(jnp.float32)[0:1]
        at = pl.ds(pl.multiple_of((codes[c] & 1) * BLK, BLK), BLK)
        value = block_ref[c, 0:BLK, :].astype(jnp.float32) * scale
        spread[c * BLK : (c + 1) * BLK, at] = value.astype(jnp.bfloat16)
    number = 0
    for sum_ref, picked_ref in ((s0, p0), (s1, p1), (s2, p2)):
        delta = jnp.dot(picked_ref[...], spread[...], preferred_element_type=jnp.float32)
        total = (sum_ref[...].astype(jnp.float32) + delta).astype(jnp.bfloat16)
        for n in range(sum_ref.shape[0] // BLK):
            second, first = TURNS[number // SIDE], number % SIDE
            number += 1
            along_y = (x + SIDE - second) % SIDE * SIDE + first
            along_x = first * SIDE + (y + SIDE - second) % SIDE
            to = jnp.where(core == 0, along_y, along_x)
            out_ref[to] = total[n * BLK : (n + 1) * BLK, :]


def shards(
    learn_hidden,
    learn_cotangent,
    master_blocks,
    changed,
    rollout_slot,
    rollout_weight,
    rollout_scale,
    decode_hidden,
    decode_routes,
    decode_gates,
):
    dp_count = lax.axis_size("dp")
    exp_dev, learn_rows, width_ff = learn_hidden.shape[1:]
    width_local = rollout_weight.shape[2]
    per_group = master_blocks.shape[2]
    tokens = decode_hidden.shape[0] * decode_hidden.shape[1]
    rows = SIDE * tokens
    limit = pltpu.CompilerParams(vmem_limit_bytes=32 * 1024 * 1024)
    whole = pltpu.CompilerParams(vmem_limit_bytes=60 * 1024 * 1024)
    table = jnp.transpose(changed, (1, 2, 0))

    token_args = (
        decode_hidden,
        jnp.transpose(decode_routes, (0, 2, 1)),
        jnp.transpose(decode_gates, (0, 2, 1)),
    )
    chunk = pl.pallas_call(
        chunk_kernel,
        out_shape=jax.ShapeDtypeStruct((SIDE, width_ff + EXTRA, BLK), jnp.bfloat16),
        in_specs=[smem()] + [pl.BlockSpec(memory_space=ANY)] * 3,
        out_specs=vmem(),
        scratch_shapes=[pltpu.VMEM(a.shape, a.dtype) for a in token_args]
        + [pltpu.SemaphoreType.DMA((3,))],
        compiler_params=whole,
    )(rollout_slot, *token_args)
    chunk, learn_hidden, learn_cotangent, rollout_weight = lax.optimization_barrier(
        (chunk, learn_hidden, learn_cotangent, rollout_weight)
    )
    line = lax.all_to_all(chunk, "expert", 0, 0, axis_index_groups=lines(), tiled=True)

    tiles = pl.pallas_call(
        select_kernel,
        out_shape=jax.ShapeDtypeStruct((dp_count, per_group, 2, learn_rows, BLK), jnp.bfloat16),
        in_specs=[smem()] + [pl.BlockSpec(memory_space=ANY)] * 2,
        out_specs=vmem(),
        scratch_shapes=[
            pltpu.VMEM(learn_hidden.shape[1:], jnp.bfloat16),
            pltpu.VMEM(learn_cotangent.shape[1:], jnp.bfloat16),
            pltpu.SemaphoreType.DMA((2,)),
        ],
        compiler_params=whole,
    )(table, learn_hidden[0], learn_cotangent[0])
    tiles, rollout_scale = lax.optimization_barrier((tiles, rollout_scale))
    scales = lax.all_gather(
        rollout_scale, "expert", axis_index_groups=both_cores(), tiled=True
    )
    line, tiles, scales = lax.optimization_barrier((line, tiles, scales))
    received = lax.all_to_all(tiles, "dp", 0, 0, tiled=True)

    right = lax.ppermute(line, "expert", shifted(1, 1))
    left = lax.ppermute(line, "expert", shifted(1, -1))
    far = lax.ppermute(right, "expert", shifted(1, 1))

    other_weight = lax.ppermute(rollout_weight, "expert", core_swap())
    scales = scales.astype(jnp.float32).reshape(CORES * exp_dev, -1)

    def cost(lines):
        return pl.CostEstimate(
            flops=lines * 2 * rows * width_ff * width_local * 8,
            bytes_accessed=lines * 6 * 1024 * 1024,
            transcendentals=0,
        )

    def sums_of(lines):
        return (
            jax.ShapeDtypeStruct((lines * rows, width_local), jnp.bfloat16),
            jax.ShapeDtypeStruct((lines * rows, 4 * BLK), jnp.bfloat16),
        )

    held = CORES * exp_dev
    weights, sum_first, picked_first = pl.pallas_call(
        first_kernel,
        out_shape=(jax.ShapeDtypeStruct((held,) + rollout_weight.shape[1:], jnp.bfloat16),)
        + sums_of(2),
        in_specs=[smem()] * 3 + [vmem()] * 4,
        out_specs=(vmem(),) * 3,
        scratch_shapes=[pltpu.SMEM((held + 1, 16), jnp.float32)],
        compiler_params=limit,
        cost_estimate=cost(2),
    )(table, rollout_slot, scales, rollout_weight, other_weight, line, right)

    def add_line(piece):
        return pl.pallas_call(
            line_kernel,
            out_shape=sums_of(1),
            in_specs=[smem()] * 2 + [vmem()] * 2,
            out_specs=(vmem(),) * 2,
            compiler_params=limit,
            cost_estimate=cost(1),
        )(table, rollout_slot, weights, piece)

    left, sum_first = lax.optimization_barrier((left, sum_first))
    sum_left, picked_left = add_line(left)
    far, sum_left = lax.optimization_barrier((far, sum_left))
    sum_far, picked_far = add_line(far)
    received, sum_far = lax.optimization_barrier((received, sum_far))

    step_size = learning_rate / math.sqrt(dp_count * learn_rows)
    own_block = pl.pallas_call(
        functools.partial(refresh_kernel, step_size=step_size),
        out_shape=jax.ShapeDtypeStruct((per_group, BLK + 16, BLK), jnp.bfloat16),
        in_specs=[vmem(), vmem()],
        out_specs=vmem(),
        compiler_params=limit,
    )(received, master_blocks[0, 0])
    blocks = lax.all_gather(own_block, "expert", axis_index_groups=both_cores(), tiled=True)

    outgoing = pl.pallas_call(
        last_kernel,
        out_shape=jax.ShapeDtypeStruct((SIDE * SIDE, tokens, width_local), jnp.bfloat16),
        in_specs=[smem()] * 2 + [vmem()] * 7,
        out_specs=vmem(),
        scratch_shapes=[pltpu.VMEM((4 * BLK, width_local), jnp.bfloat16)],
        compiler_params=limit,
    )(
        table, rollout_slot, blocks,
        sum_first, sum_left, sum_far, picked_first, picked_left, picked_far,
    )

    returned = lax.all_to_all(
        outgoing, "expert", 0, 0, axis_index_groups=same_core(), tiled=True
    )
    result = jnp.sum(returned.astype(jnp.float32), axis=0).astype(jnp.bfloat16)
    return result.reshape(decode_hidden.shape[0], decode_hidden.shape[1], width_local)


def solution(mesh):
    return jax.shard_map(
        shards,
        mesh=mesh,
        in_specs=(
            P("dp", "expert", None, None),
            P("dp", "expert", None, None),
            P("expert", "dp", None, None, None),
            P(),
            P(),
            P("expert", None, "dp"),
            P("expert", None, "dp"),
            P(None, "expert", None),
            P(None, "expert", None),
            P(None, "expert", None),
        ),
        out_specs=P(None, "expert", "dp"),
        check_vma=False,
    )
```
